32 devices in a mesh: replica: 2 (over x), patch: 8 (over z, y), band: 2 (over core).
Axes of the slice: x: 2, y: 2, z: 4, core: 2. Of those that a mesh axis runs over, the one named last changes fastest.
Arguments:
- grid_latent: bfloat16 [32768, 512], P(('replica', 'patch', 'band')), parts along dimension 0, may hold values from -6 to 6
- mesh_latent: bfloat16 [8192, 512], P(('replica', 'patch', 'band')), parts along dimension 0, may hold values from -6 to 6
- edge_features: bfloat16 [4, 32768], P(None, ('replica', 'patch', 'band')), parts along dimension 1, may hold values from -6 to 6
- edge_sender: int32 [32768], P(('replica', 'patch', 'band')), parts along dimension 0, may hold values from 0 to 1023
- edge_receiver: int32 [32768], P(('replica', 'patch', 'band')), parts along dimension 0, may hold values from 0 to 255
- block_offset: int32 [256], P(('replica', 'patch', 'band')), parts along dimension 0, may hold values from -2 to 2, as said below
- link_latent: bfloat16 [32768, 512], P(('replica', 'patch', 'band')), parts along dimension 0, may hold values from -6 to 6
- link_sender: int32 [32768], P(('replica', 'patch', 'band')), parts along dimension 0, may hold values from 0 to 4095, as said below
- link_receiver: int32 [32768], P(('replica', 'patch', 'band')), parts along dimension 0, may hold values from 0 to 255
- feature_weight: bfloat16 [4, 512], replicated, may hold values from -3 to 3
- source_weight: bfloat16 [512, 512], replicated, may hold values from -0.25 to 0.25
- target_weight: bfloat16 [512, 512], replicated, may hold values from -0.25 to 0.25
- edge_weight: bfloat16 [512, 512], replicated, may hold values from -0.25 to 0.25
- edge_second: bfloat16 [512, 512], replicated, may hold values from -0.25 to 0.25
- node_first: bfloat16 [512, 512], replicated, may hold values from -0.25 to 0.25
- node_summed: bfloat16 [512, 512], replicated, may hold values from -0.25 to 0.25
- node_second: bfloat16 [512, 512], replicated, may hold values from -0.25 to 0.25
- link_weight: bfloat16 [512, 512], replicated, may hold values from -0.25 to 0.25
- link_source: bfloat16 [512, 512], replicated, may hold values from -0.25 to 0.25
- link_target: bfloat16 [512, 512], replicated, may hold values from -0.25 to 0.25
- link_second: bfloat16 [512, 512], replicated, may hold values from -0.25 to 0.25
- vertex_first: bfloat16 [512, 512], replicated, may hold values from -0.25 to 0.25
- vertex_summed: bfloat16 [512, 512], replicated, may hold values from -0.25 to 0.25
- vertex_second: bfloat16 [512, 512], replicated, may hold values from -0.25 to 0.25
Outputs:
- mesh_out: bfloat16 [8192, 512], P(('replica', 'patch', 'band')), parts along dimension 0
The draws below stay inside these ranges and needn't reach their ends.
There are 2 independent parts, one for each index of `replica`. The reference program is written for one: setup_inputs(seed, part) draws one part's arguments, and reference() takes and returns one part's arrays. A program takes and returns all parts, laid end to end along the dimension named above; an argument that names none is the same for every part. Nothing has to cross between parts.
Inputs may be any that keep to these rules, and one draw needn't show every extreme that they name: `block_offset`: at most 3 blocks of one device name the same offset, and on every device some offset is named by exactly 3 blocks. `link_sender`: the sender of a mesh edge lies on a device at most 2 positions away, cyclically along patch+band, from the edge's device.
All inputs are finite; a program needn't handle non-finite values.
Results may differ from the reference program's by a relative error of at most 0.014.
Values may be sent and summed in bfloat16 or wider, within the bound.
A program may use at most 64 MiB of HBM per device.

```python
import jax
import jax.numpy as jnp
from jax import lax

LATENT = 512
EDGE_FEATS = 4
REACH = 2
BLOCK = 128
GRID_DEV = 1024
MESH_DEV = 256
G2M_DEV = 1024
M_EDGE_DEV = 1024
PIECES = 16
BLOCKS = 8
CAP_BLOCKS = 3
GRID = 16384
MESH = 4096
G2M = 16384
M_EDGES = 16384


def draw_block_offset(key, part):
    key = jax.random.fold_in(key, 11)
    width_span = 2 * REACH + 1
    device_keys = jax.random.split(key, PIECES)

    def one_device(device_key):
        first_key, second_key, third_key = jax.random.split(device_key, 3)
        crowded = jax.random.randint(first_key, (), 0, width_span)
        remaining = BLOCKS - CAP_BLOCKS
        capacity = 2 * REACH * (CAP_BLOCKS - 1)
        chosen = jax.random.permutation(second_key, capacity)[:remaining]
        others = (chosen // (CAP_BLOCKS - 1)).astype(jnp.int32)
        others = others + (others >= crowded).astype(jnp.int32)
        labels = jnp.concatenate([jnp.full((CAP_BLOCKS,), crowded, jnp.int32), others])
        shuffle = jax.random.permutation(third_key, BLOCKS)
        return labels[shuffle] - REACH
    return jax.vmap(one_device)(device_keys).reshape(-1).astype(jnp.int32)


def draw_link_sender(key, part):
    key = jax.random.fold_in(key, 23)
    first_key, second_key = jax.random.split(key)
    total_rows = M_EDGE_DEV * PIECES
    resident = jnp.arange(total_rows, dtype=jnp.int32) // M_EDGE_DEV
    moves = jax.random.randint(first_key, (total_rows,), -REACH, REACH + 1)
    owner = (resident + moves + PIECES) % PIECES
    return (owner * MESH_DEV + jax.random.randint(second_key, (total_rows,), 0, MESH_DEV)).astype(jnp.int32)


def place_ends(array, stream_key, low, high):
    longest = array.shape.index(max(array.shape))
    spots = []
    for shift in (0, 1):
        where = [jax.random.randint(jax.random.fold_in(stream_key, axis), (), 0, length) for axis, length in enumerate(array.shape)]
        where[longest] = (where[longest] + shift) % array.shape[longest]
        spots.append(tuple(where))
    return array.at[spots[0]].set(low).at[spots[1]].set(high)


def block_levels(rng, shape, pieces, least, high):
    factor_of = 1.0
    for axis_at, shards_of in pieces:
        steps = jax.random.uniform(jax.random.fold_in(jax.random.fold_in(rng, 6), axis_at), (shards_of,), jnp.float32, least / len(pieces), high / len(pieces))
        factor_of = factor_of * jnp.repeat(jnp.exp(steps), shape[axis_at] // shards_of).reshape((-1,) + (1,) * (len(shape) - 1 - axis_at))
    return factor_of


def scatter_about(key, dims, deviation, limit, cuts=(), kind=jnp.bfloat16):
    values = deviation * jax.random.normal(key, dims, jnp.float32)
    if cuts:
        values = values * block_levels(key, dims, cuts, -0.22, 0.18)
    return jnp.clip(values, -limit, limit).astype(kind)


def setup_inputs(seed: int = 0, part: int = 0) -> dict:
    splits = jax.random.split(jax.random.key(seed), 25)
    own_keys = jax.random.split(jax.random.fold_in(splits[24], part), 25)
    return {
        "grid_latent": scatter_about(own_keys[0], (GRID, LATENT), 1.0, 6.0, ((0, 16),)),
        "mesh_latent": scatter_about(own_keys[1], (MESH, LATENT), 1.0, 6.0, ((0, 16),)),
        "edge_features": scatter_about(own_keys[2], (EDGE_FEATS, G2M), 1.0, 6.0, ((1, 16),)),
        "edge_sender": place_ends(jax.random.randint(own_keys[3], (G2M,), 0, GRID_DEV), jax.random.fold_in(own_keys[3], 1), 0, GRID_DEV - 1).astype(jnp.int32),
        "edge_receiver": place_ends(jax.random.randint(own_keys[4], (G2M,), 0, MESH_DEV), jax.random.fold_in(own_keys[4], 1), 0, MESH_DEV - 1).astype(jnp.int32),
        "block_offset": draw_block_offset(jax.random.fold_in(jax.random.fold_in(splits[24], part), 71), part),
        "link_latent": scatter_about(own_keys[6], (M_EDGES, LATENT), 1.0, 6.0, ((0, 16),)),
        "link_sender": draw_link_sender(jax.random.fold_in(jax.random.fold_in(splits[24], part), 71), part),
        "link_receiver": place_ends(jax.random.randint(own_keys[8], (M_EDGES,), 0, MESH_DEV), jax.random.fold_in(own_keys[8], 1), 0, MESH_DEV - 1).astype(jnp.int32),
        "feature_weight": scatter_about(splits[9], (EDGE_FEATS, LATENT), EDGE_FEATS ** -0.5, 3.0),
        "source_weight": scatter_about(splits[10], (LATENT, LATENT), LATENT ** -0.5, 0.25),
        "target_weight": scatter_about(splits[11], (LATENT, LATENT), LATENT ** -0.5, 0.25),
        "edge_weight": scatter_about(splits[12], (LATENT, LATENT), LATENT ** -0.5, 0.25),
        "edge_second": scatter_about(splits[13], (LATENT, LATENT), LATENT ** -0.5, 0.25),
        "node_first": scatter_about(splits[14], (LATENT, LATENT), LATENT ** -0.5, 0.25),
        "node_summed": scatter_about(splits[15], (LATENT, LATENT), LATENT ** -0.5, 0.25),
        "node_second": scatter_about(splits[16], (LATENT, LATENT), LATENT ** -0.5, 0.25),
        "link_weight": scatter_about(splits[17], (LATENT, LATENT), LATENT ** -0.5, 0.25),
        "link_source": scatter_about(splits[18], (LATENT, LATENT), LATENT ** -0.5, 0.25),
        "link_target": scatter_about(splits[19], (LATENT, LATENT), LATENT ** -0.5, 0.25),
        "link_second": scatter_about(splits[20], (LATENT, LATENT), LATENT ** -0.5, 0.25),
        "vertex_first": scatter_about(splits[21], (LATENT, LATENT), LATENT ** -0.5, 0.25),
        "vertex_summed": scatter_about(splits[22], (LATENT, LATENT), LATENT ** -0.5, 0.25),
        "vertex_second": scatter_about(splits[23], (LATENT, LATENT), LATENT ** -0.5, 0.25),
    }


EPSILON = 1e-05

def normalize(values):
    average = lax.optimization_barrier(jnp.mean(values, axis=-1, keepdims=True))
    centred = values - average
    spread = lax.optimization_barrier(jnp.mean(centred * centred, axis=-1, keepdims=True))
    return centred * lax.rsqrt(spread + EPSILON)

def project(left, right):
    return jnp.dot(left, right, preferred_element_type=jnp.float32)

def edge_update(base, before, second):
    hidden = jax.nn.silu(before).astype(jnp.bfloat16)
    return (base.astype(jnp.float32) + normalize(project(hidden, second))).astype(jnp.bfloat16)

def node_update(nodes, summed, first, summed_weight, second):
    before = project(nodes, first) + project(summed.astype(jnp.bfloat16), summed_weight)
    hidden = jax.nn.silu(before).astype(jnp.bfloat16)
    return (nodes.astype(jnp.float32) + normalize(project(hidden, second))).astype(jnp.bfloat16)

def reference(grid_latent, mesh_latent, edge_features, edge_sender, edge_receiver, block_offset, link_latent, link_sender, link_receiver, feature_weight, source_weight, target_weight, edge_weight, edge_second, node_first, node_summed, node_second, link_weight, link_source, link_target, link_second, vertex_first, vertex_summed, vertex_second):
    mesh_total = MESH_DEV * PIECES
    source_proj = project(grid_latent, source_weight).astype(jnp.bfloat16)
    target_proj = project(mesh_latent, target_weight).astype(jnp.bfloat16)

    def one_piece(total, position):
        start = (position * G2M_DEV).astype(jnp.int32)
        senders = lax.dynamic_slice_in_dim(edge_sender, start, G2M_DEV) + position * GRID_DEV
        receivers = lax.dynamic_slice_in_dim(edge_receiver, start, G2M_DEV)
        offsets = jnp.repeat(lax.dynamic_slice_in_dim(block_offset, (position * BLOCKS).astype(jnp.int32), BLOCKS), BLOCK)
        owner = (position + offsets + PIECES) % PIECES
        targets = (owner * MESH_DEV + receivers).astype(jnp.int32)
        features = lax.dynamic_slice_in_dim(edge_features, start, G2M_DEV, 1)
        embedded = project(features.T, feature_weight).astype(jnp.bfloat16)
        before = project(embedded, edge_weight) + source_proj[senders].astype(jnp.float32) + target_proj[targets].astype(jnp.float32)
        updated = edge_update(embedded, before, edge_second)
        return (total + jax.ops.segment_sum(updated.astype(jnp.float32), targets, mesh_total), None)
    summed, _ = lax.scan(one_piece, jnp.zeros((mesh_total, LATENT), jnp.float32), jnp.arange(PIECES, dtype=jnp.int32))
    mesh_next = node_update(mesh_latent, summed, node_first, node_summed, node_second)
    link_src = project(mesh_next, link_source).astype(jnp.bfloat16)
    link_dst = project(mesh_next, link_target).astype(jnp.bfloat16)
    owners = jnp.arange(M_EDGE_DEV * PIECES, dtype=jnp.int32) // M_EDGE_DEV
    link_targets = (owners * MESH_DEV + link_receiver).astype(jnp.int32)
    before = project(link_latent, link_weight) + link_src[link_sender].astype(jnp.float32) + link_dst[link_targets].astype(jnp.float32)
    link_new = edge_update(link_latent, before, link_second)
    link_sum = jax.ops.segment_sum(link_new.astype(jnp.float32), link_targets, mesh_total)
    return node_update(mesh_next, link_sum, vertex_first, vertex_summed, vertex_second)
```

```python
import functools

import jax
import jax.numpy as jnp
from jax import lax
from jax.experimental import pallas as pl
from jax.experimental.pallas import tpu as pltpu
from jax.sharding import PartitionSpec as P

REACH = 2
BLOCK = 128
EPSILON = 1e-05
CHUNKS = 2
TILE = 256
LANES = 128
AXES = ("replica", "patch", "band")
BF16 = jnp.bfloat16
F32 = jnp.float32

WEIGHTS = 14


def mm(left, right):
    return jnp.dot(left, right, preferred_element_type=F32)


def silu(value):
    half = 0.5 * value
    return half + half * jnp.tanh(half)


def normalize(values):
    average = jnp.mean(values, axis=-1, keepdims=True)
    centred = values - average
    spread = jnp.mean(centred * centred, axis=-1, keepdims=True)
    return centred * lax.rsqrt(spread + EPSILON)


def as_columns(row):
    return jnp.transpose(jnp.broadcast_to(row, (LANES, LANES)))


def one_hot_rows(keys, width):
    parts = []
    for at in range(keys.shape[1] // LANES):
        columns = as_columns(keys[:, at * LANES : (at + 1) * LANES])
        wide = jnp.concatenate([columns] * (width // LANES), axis=1)
        ids = lax.broadcasted_iota(jnp.int32, (LANES, width), 1)
        parts.append(jnp.where(wide == ids, 1.0, 0.0).astype(BF16))
    return jnp.concatenate(parts, axis=0)


def one_hot_columns(keys, first, height):
    ids = lax.broadcasted_iota(jnp.int32, (height, keys.shape[1]), 0)
    return jnp.where(jnp.broadcast_to(keys - first, ids.shape) == ids, 1.0, 0.0).astype(BF16)


def kernel(
    patches,
    feat_ref, sender_ref, receiver_ref, offset_ref, link_sender_ref, link_receiver_ref, fw_ref,
    grid_hbm, mesh_hbm, link_hbm, *rest,
):
    weights_hbm = rest[:WEIGHTS]
    out_ref = rest[WEIGHTS]
    (
        grid, mesh, link, weights,
        tab1, tab2, src, emb, pre, link_pre, fresh,
        sib_out, sib_in, z_out, z_in, y_out, y_in, y_own, m_own, mesh_next, link_dst,
        in_sems, ex_send, ex_recv, sib_send, sib_recv, z_send, z_recv, y_send, y_recv,
    ) = rest[WEIGHTS + 1 :]
    rows = mesh.shape[0]
    edges = fresh.shape[0]
    span = 2 * REACH + 1
    part = rows // CHUNKS
    chip = lax.axis_index("patch")
    core = lax.axis_index("band")
    odd = lax.rem(chip, 2)
    partner = chip + 1 - 2 * odd
    up = lax.rem(chip + 2, patches)
    down = lax.rem(chip + patches - 2, patches)
    cast_to = up * (1 - odd) + down * odd
    fold_to = down * (1 - odd) + up * odd
    to_sib = {"patch": chip, "band": 1 - core}
    to_partner = {"patch": partner, "band": core}
    to_cast = {"patch": cast_to, "band": core}
    to_fold = {"patch": fold_to, "band": core}

    barrier = pltpu.get_barrier_semaphore()
    for where in (to_sib, to_partner, to_cast, to_fold):
        pl.semaphore_signal(barrier, inc=1, device_id=where, device_id_type=pl.DeviceIdType.MESH)

    loads = [
        pltpu.make_async_copy(weights_hbm[at], weights.at[at], in_sems.at[at])
        for at in range(WEIGHTS)
    ]
    (w_target, w_source, w_edge, w_edge2, w_first, w_summed, w_second,
     w_link, w_lsrc, w_ldst, w_link2, w_vfirst, w_vsummed, w_vsecond) = range(WEIGHTS)
    load_grid = pltpu.make_async_copy(grid_hbm, grid, in_sems.at[WEIGHTS])
    load_mesh = pltpu.make_async_copy(mesh_hbm, mesh, in_sems.at[WEIGHTS + 1])
    load_link = pltpu.make_async_copy(link_hbm, link, in_sems.at[WEIGHTS + 2])
    load_mesh.start()
    loads[w_target].start()
    load_grid.start()
    for at in (w_source, w_edge, w_edge2):
        loads[at].start()
    load_link.start()
    for at in range(w_first, WEIGHTS):
        loads[at].start()

    def remote(source, target, send, recv, where):
        return pltpu.make_async_remote_copy(
            src_ref=source, dst_ref=target, send_sem=send, recv_sem=recv,
            device_id=where, device_id_type=pl.DeviceIdType.MESH,
        )

    class Multicast:
        def __init__(self, tab, which):
            def slot(index, at):
                return tab.at[pl.ds(pl.multiple_of(index * rows + at * part, part), part)]

            def sems(at):
                return ex_send.at[which, at], ex_recv.at[which, at]

            own = 2 + core
            there = 4 * odd + core
            from_partner = 4 * (1 - odd) + core
            from_far = 4 * odd + core
            self.own, self.y, self.z, self.ysib, self.zsib = [], [], [], [], []
            for at in range(CHUNKS):
                base = 5 * at
                self.own.append(remote(slot(own, at), slot(own, at), *sems(base), to_sib))
                self.y.append(remote(slot(own, at), slot(there, at), *sems(base + 1), to_partner))
                self.z.append(remote(slot(from_partner, at), slot(there, at), *sems(base + 2), to_cast))
                self.ysib.append(remote(slot(from_partner, at), slot(from_partner, at), *sems(base + 3), to_sib))
                self.zsib.append(remote(slot(from_far, at), slot(from_far, at), *sems(base + 4), to_sib))

        def start(self):
            for at in range(CHUNKS):
                self.y[at].start()
            for at in range(CHUNKS):
                self.own[at].start()

        def relay(self):
            for at in range(CHUNKS):
                self.y[at].wait_recv()
                self.z[at].start()
                self.ysib[at].start()

        def finish(self):
            for at in range(CHUNKS):
                self.z[at].wait_recv()
                self.zsib[at].start()
            for at in range(CHUNKS):
                self.own[at].wait_recv()
                self.ysib[at].wait_recv()
                self.zsib[at].wait_recv()

        def drain(self):
            for at in range(CHUNKS):
                for copy in (self.own[at], self.y[at], self.z[at], self.ysib[at], self.zsib[at]):
                    copy.wait_send()

    def tiles(count, step):
        def go(at, carry):
            step(pl.ds(pl.multiple_of(at * TILE, TILE), TILE))
            return carry

        lax.fori_loop(0, count // TILE, go, 0)

    own_rows = pl.ds(pl.multiple_of((2 + core) * rows, rows), rows)
    near = pl.ds(pl.multiple_of(core * rows, rows), span * rows)
    load_mesh.wait()
    loads[w_target].wait()
    tab1[own_rows, :] = mm(mesh[...], weights[w_target]).astype(BF16)
    pl.semaphore_wait(barrier, 4)
    cast1 = Multicast(tab1, 0)
    cast1.start()

    keys = []
    for at in range(edges // BLOCK):
        keys.append(
            receiver_ref[:, at * BLOCK : (at + 1) * BLOCK] + (offset_ref[at] + REACH) * rows
        )
    edge_key = jnp.concatenate(keys, axis=1)

    load_grid.wait()
    loads[w_source].wait()

    def project_source(at):
        src[at, :] = mm(grid[at, :], weights[w_source]).astype(BF16)

    tiles(src.shape[0], project_source)
    emb[...] = lax.dot_general(
        feat_ref[...], fw_ref[...], (((0,), (0,)), ((), ())), preferred_element_type=F32
    ).astype(BF16)
    cast1.relay()
    loads[w_edge].wait()
    for at in range(edges // TILE):
        here = pl.ds(at * TILE, TILE)
        hot = one_hot_rows(sender_ref[:, at * TILE : (at + 1) * TILE], src.shape[0])
        pre[here, :] = mm(emb[here, :], weights[w_edge]) + mm(hot, src[...])
    loads[w_edge2].wait()
    cast1.finish()

    for at in range(edges // TILE):
        here = pl.ds(at * TILE, TILE)
        hot = one_hot_rows(edge_key[:, at * TILE : (at + 1) * TILE], span * rows)
        hidden = silu(pre[here, :] + mm(hot, tab1[near, :])).astype(BF16)
        fresh[here, :] = (
            emb[here, :].astype(F32) + normalize(mm(hidden, weights[w_edge2]))
        ).astype(BF16)
    cast1.drain()

    jz = 2 * odd
    jy = 2 * (1 - odd)
    slot_key = edge_key + core * rows

    def partial(slot):
        return mm(one_hot_columns(slot_key, slot * rows, rows), fresh[...])

    order = (jz, jy, 1)
    sibs = []
    for at in range(3):
        sib_out[at] = partial(2 * order[at] + 1 - core).astype(BF16)
        copy = remote(sib_out.at[at], sib_in.at[at], sib_send.at[at], sib_recv.at[at], to_sib)
        copy.start()
        sibs.append(copy)
        if at == 0:
            far = partial(2 * jz + core)
            copy.wait_recv()
            z_out[...] = (far + sib_in[0].astype(F32)).astype(BF16)
            z_copies = []
            for chunk in range(CHUNKS):
                piece = pl.ds(chunk * part, part)
                z_copies.append(
                    remote(z_out.at[piece], z_in.at[piece], z_send.at[chunk], z_recv.at[chunk], to_fold)
                )
                z_copies[-1].start()
    y_own[...] = partial(2 * jy + core)
    m_own[...] = partial(2 + core)
    sibs[1].wait_recv()
    y_own[...] += sib_in[1].astype(F32)
    sibs[2].wait_recv()
    m_own[...] += sib_in[2].astype(F32)
    y_copies = []
    for chunk in range(CHUNKS):
        piece = pl.ds(chunk * part, part)
        z_copies[chunk].wait_recv()
        y_out[piece, :] = (y_own[piece, :] + z_in[piece, :].astype(F32)).astype(BF16)
        y_copies.append(
            remote(y_out.at[piece], y_in.at[piece], y_send.at[chunk], y_recv.at[chunk], to_partner)
        )
        y_copies[-1].start()
    load_link.wait()
    loads[w_link].wait()

    def project_link(at):
        link_pre[at, :] = mm(link[at, :], weights[w_link])

    tiles(edges, project_link)
    for at in (w_first, w_summed, w_second, w_lsrc, w_ldst, w_link2, w_vfirst, w_vsummed, w_vsecond):
        loads[at].wait()
    node_pre = mm(mesh[...], weights[w_first])
    for chunk in range(CHUNKS):
        y_copies[chunk].wait_recv()
    summed = (m_own[...] + y_in[...].astype(F32)).astype(BF16)
    hidden = silu(node_pre + mm(summed, weights[w_summed])).astype(BF16)
    mesh_next[...] = (
        mesh[...].astype(F32) + normalize(mm(hidden, weights[w_second]))
    ).astype(BF16)
    for copy in sibs + z_copies + y_copies:
        copy.wait_send()

    tab2[own_rows, :] = mm(mesh_next[...], weights[w_lsrc]).astype(BF16)
    cast2 = Multicast(tab2, 1)
    cast2.start()
    link_dst[...] = mm(mesh_next[...], weights[w_ldst]).astype(BF16)
    for at in range(edges // TILE):
        here = pl.ds(at * TILE, TILE)
        hot = one_hot_rows(link_receiver_ref[:, at * TILE : (at + 1) * TILE], rows)
        link_pre[here, :] += mm(hot, link_dst[...])
        if at == 1:
            cast2.relay()
    y_own[...] = mm(mesh_next[...], weights[w_vfirst])
    total = 2 * patches
    bits = rows.bit_length() - 1
    sender = link_sender_ref[...]
    place = lax.shift_right_logical(sender, bits) - (2 * chip + core) + REACH
    place = jnp.where(place < 0, place + total, place)
    place = jnp.where(place >= total, place - total, place)
    link_key = place * rows + lax.bitwise_and(sender, rows - 1)
    cast2.finish()

    for at in range(edges // TILE):
        here = pl.ds(at * TILE, TILE)
        hot = one_hot_rows(link_key[:, at * TILE : (at + 1) * TILE], span * rows)
        hidden = silu(link_pre[here, :] + mm(hot, tab2[near, :])).astype(BF16)
        fresh[here, :] = (
            link[here, :].astype(F32) + normalize(mm(hidden, weights[w_link2]))
        ).astype(BF16)
    link_sum = mm(one_hot_columns(link_receiver_ref[...], 0, rows), fresh[...]).astype(BF16)
    hidden = silu(y_own[...] + mm(link_sum, weights[w_vsummed])).astype(BF16)
    out_ref[...] = (
        mesh_next[...].astype(F32) + normalize(mm(hidden, weights[w_vsecond]))
    ).astype(BF16)
    cast2.drain()


def body(
    patches,
    grid_latent, mesh_latent, edge_features, edge_sender, edge_receiver, block_offset,
    link_latent, link_sender, link_receiver, feature_weight, source_weight, target_weight,
    edge_weight, edge_second, node_first, node_summed, node_second, link_weight, link_source,
    link_target, link_second, vertex_first, vertex_summed, vertex_second,
):
    rows, width = mesh_latent.shape
    edges = edge_sender.shape[0]
    vmem = pl.BlockSpec(memory_space=pltpu.VMEM)
    smem = pl.BlockSpec(memory_space=pltpu.SMEM)
    anywhere = pl.BlockSpec(memory_space=pl.ANY)
    dma = pltpu.SemaphoreType.DMA
    table = pltpu.VMEM((6 * rows, width), BF16)
    flat = pltpu.VMEM((rows, width), BF16)
    return pl.pallas_call(
        functools.partial(kernel, patches),
        out_shape=jax.ShapeDtypeStruct((rows, width), BF16),
        in_specs=[vmem, vmem, vmem, smem, vmem, vmem, vmem] + [anywhere] * (3 + WEIGHTS),
        out_specs=vmem,
        scratch_shapes=[
            pltpu.VMEM(grid_latent.shape, BF16),
            flat,
            pltpu.VMEM(link_latent.shape, BF16),
            pltpu.VMEM((WEIGHTS, width, width), BF16),
            table,
            table,
            pltpu.VMEM((grid_latent.shape[0], width), BF16),
            pltpu.VMEM((edges, width), BF16),
            pltpu.VMEM((edges, width), F32),
            pltpu.VMEM((edges, width), F32),
            pltpu.VMEM((edges, width), BF16),
            pltpu.VMEM((3, rows, width), BF16),
            pltpu.VMEM((3, rows, width), BF16),
            flat, flat, flat, flat,
            pltpu.VMEM((rows, width), F32),
            pltpu.VMEM((rows, width), F32),
            flat, flat,
            dma((WEIGHTS + 3,)),
            dma((2, 5 * CHUNKS)), dma((2, 5 * CHUNKS)),
            dma((3,)), dma((3,)),
            dma((CHUNKS,)), dma((CHUNKS,)),
            dma((CHUNKS,)), dma((CHUNKS,)),
        ],
        compiler_params=pltpu.CompilerParams(
            collective_id=0, has_side_effects=True, vmem_limit_bytes=48 * 1024 * 1024
        ),
    )(
        edge_features, edge_sender.reshape(1, -1), edge_receiver.reshape(1, -1), block_offset,
        link_sender.reshape(1, -1), link_receiver.reshape(1, -1), feature_weight,
        grid_latent, mesh_latent, link_latent,
        target_weight, source_weight, edge_weight, edge_second, node_first, node_summed,
        node_second, link_weight, link_source, link_target, link_second, vertex_first,
        vertex_summed, vertex_second,
    )


def solution(mesh):
    rows = P(AXES, None)
    flat = P(AXES)
    placed = (rows, rows, P(None, AXES), flat, flat, flat, rows, flat, flat) + (P(),) * 15
    return jax.shard_map(
        functools.partial(body, mesh.shape["patch"]),
        mesh=mesh,
        in_specs=placed,
        out_specs=rows,
        check_vma=False,
    )
```

```python
import functools

import jax
import jax.numpy as jnp
from jax import lax
from jax.experimental import pallas as pl
from jax.experimental.pallas import tpu as pltpu
from jax.sharding import PartitionSpec as P

REACH = 2
BLOCK = 128
EPSILON = 1e-05
CHUNKS = 4
TILE = 512
LANES = 128
AXES = ("replica", "patch", "band")
BF16 = jnp.bfloat16
F32 = jnp.float32

WEIGHTS = 14


def mm(left, right):
    return jnp.dot(left, right, preferred_element_type=F32)


def silu(value):
    half = 0.5 * value
    return half + half * jnp.tanh(half)


def normalize(values):
    average = jnp.mean(values, axis=-1, keepdims=True)
    centred = values - average
    spread = jnp.mean(centred * centred, axis=-1, keepdims=True)
    return centred * lax.rsqrt(spread + EPSILON)


def as_columns(row):
    return jnp.transpose(jnp.broadcast_to(row, (LANES, LANES)))


def one_hot_rows(keys, width):
    parts = []
    for at in range(keys.shape[1] // LANES):
        columns = as_columns(keys[:, at * LANES : (at + 1) * LANES])
        wide = jnp.concatenate([columns] * (width // LANES), axis=1)
        ids = lax.broadcasted_iota(jnp.int32, (LANES, width), 1)
        parts.append(jnp.where(wide == ids, 1.0, 0.0).astype(BF16))
    return jnp.concatenate(parts, axis=0)


def one_hot_columns(keys, first, height):
    ids = lax.broadcasted_iota(jnp.int32, (height, keys.shape[1]), 0)
    return jnp.where(jnp.broadcast_to(keys - first, ids.shape) == ids, 1.0, 0.0).astype(BF16)


def kernel(
    patches,
    feat_ref, sender_ref, receiver_ref, offset_ref, link_sender_ref, link_receiver_ref, fw_ref,
    grid_hbm, mesh_hbm, link_hbm, *rest,
):
    weights_hbm = rest[:WEIGHTS]
    out_ref = rest[WEIGHTS]
    (
        grid, mesh, link, weights,
        tab1, tab2, src, emb, pre, link_pre, fresh,
        sib_out, sib_in, z_out, z_in, y_out, y_in, z_own, y_own, m_own, mesh_next, link_dst,
        in_sems, ex_send, ex_recv, sib_send, sib_recv, z_send, z_recv, y_send, y_recv,
    ) = rest[WEIGHTS + 1 :]
    rows = mesh.shape[0]
    edges = fresh.shape[0]
    part = rows // CHUNKS
    chip = lax.axis_index("patch")
    core = lax.axis_index("band")
    odd = lax.rem(chip, 2)
    partner = chip + 1 - 2 * odd
    up = lax.rem(chip + 2, patches)
    down = lax.rem(chip + patches - 2, patches)
    cast_to = up * (1 - odd) + down * odd
    fold_to = down * (1 - odd) + up * odd
    to_sib = {"patch": chip, "band": 1 - core}
    to_partner = {"patch": partner, "band": core}
    to_cast = {"patch": cast_to, "band": core}
    to_fold = {"patch": fold_to, "band": core}

    barrier = pltpu.get_barrier_semaphore()
    for where in (to_sib, to_partner, to_cast, to_fold):
        pl.semaphore_signal(barrier, inc=1, device_id=where, device_id_type=pl.DeviceIdType.MESH)

    loads = [
        pltpu.make_async_copy(weights_hbm[at], weights.at[at], in_sems.at[at])
        for at in range(WEIGHTS)
    ]
    (w_target, w_source, w_edge, w_edge2, w_first, w_summed, w_second,
     w_link, w_lsrc, w_ldst, w_link2, w_vfirst, w_vsummed, w_vsecond) = range(WEIGHTS)
    load_grid = pltpu.make_async_copy(grid_hbm, grid, in_sems.at[WEIGHTS])
    load_mesh = pltpu.make_async_copy(mesh_hbm, mesh, in_sems.at[WEIGHTS + 1])
    load_link = pltpu.make_async_copy(link_hbm, link, in_sems.at[WEIGHTS + 2])
    load_mesh.start()
    loads[w_target].start()

    def remote(source, target, send, recv, where):
        return pltpu.make_async_remote_copy(
            src_ref=source, dst_ref=target, send_sem=send, recv_sem=recv,
            device_id=where, device_id_type=pl.DeviceIdType.MESH,
        )

    class Multicast:
        def __init__(self, tab, which):
            def slot(index, at):
                return tab.at[pl.ds(pl.multiple_of(index * rows + at * part, part), part)]

            def sems(at):
                return ex_send.at[which, at], ex_recv.at[which, at]

            own = 2 + core
            there = 4 * odd + core
            from_partner = 4 * (1 - odd) + core
            from_far = 4 * odd + core
            self.own, self.y, self.z, self.ysib, self.zsib = [], [], [], [], []
            for at in range(CHUNKS):
                base = 5 * at
                self.own.append(remote(slot(own, at), slot(own, at), *sems(base), to_sib))
                self.y.append(remote(slot(own, at), slot(there, at), *sems(base + 1), to_partner))
                self.z.append(remote(slot(from_partner, at), slot(there, at), *sems(base + 2), to_cast))
                self.ysib.append(remote(slot(from_partner, at), slot(from_partner, at), *sems(base + 3), to_sib))
                self.zsib.append(remote(slot(from_far, at), slot(from_far, at), *sems(base + 4), to_sib))

        def start(self, at):
            self.y[at].start()
            self.own[at].start()

        def relay(self, at):
            self.y[at].wait_recv()
            self.z[at].start()
            self.ysib[at].start()

        def nearby(self):
            for at in range(CHUNKS):
                self.own[at].wait_recv()
                self.ysib[at].wait_recv()

        def pass_far(self, at):
            self.z[at].wait_recv()
            self.zsib[at].start()

        def finish(self):
            for at in range(CHUNKS):
                self.zsib[at].wait_recv()

        def drain(self):
            for at in range(CHUNKS):
                for copy in (self.own[at], self.y[at], self.z[at], self.ysib[at], self.zsib[at]):
                    copy.wait_send()

    def tiles(count, step):
        def go(at, carry):
            step(pl.ds(pl.multiple_of(at * TILE, TILE), TILE))
            return carry

        lax.fori_loop(0, count // TILE, go, 0)

    own_rows = pl.ds(pl.multiple_of((2 + core) * rows, rows), rows)
    near_first = 2 * (1 - odd) * rows
    far_first = 4 * odd * rows
    near = pl.ds(pl.multiple_of(near_first, rows), 4 * rows)
    far_rows = pl.ds(pl.multiple_of(far_first, rows), 2 * rows)

    def gather_near(cast, tab, keys, total):
        cast.nearby()
        passed = 0
        for at in range(edges // TILE):
            here = pl.ds(at * TILE, TILE)
            hot = one_hot_rows(keys[:, at * TILE : (at + 1) * TILE] - near_first, 4 * rows)
            total[here, :] += mm(hot, tab[near, :])
            if passed < CHUNKS:
                cast.pass_far(passed)
                passed += 1
        for at in range(passed, CHUNKS):
            cast.pass_far(at)
        cast.finish()

    def gather_far(tab, keys, at):
        hot = one_hot_rows(keys[:, at * TILE : (at + 1) * TILE] - far_first, 2 * rows)
        return mm(hot, tab[far_rows, :])

    load_mesh.wait()
    loads[w_target].wait()
    load_grid.start()
    for at in (w_source, w_edge, w_edge2):
        loads[at].start()
    tab1[own_rows, :] = mm(mesh[...], weights[w_target]).astype(BF16)
    pl.semaphore_wait(barrier, 4)
    cast1 = Multicast(tab1, 0)
    for chunk in range(CHUNKS):
        cast1.start(chunk)

    keys = []
    for at in range(edges // BLOCK):
        keys.append(
            receiver_ref[:, at * BLOCK : (at + 1) * BLOCK] + (offset_ref[at] + REACH) * rows
        )
    slot_key = jnp.concatenate(keys, axis=1) + core * rows

    load_grid.wait()
    loads[w_source].wait()
    load_link.start()
    for at in range(w_first, WEIGHTS):
        loads[at].start()

    def project_source(at):
        src[at, :] = mm(grid[at, :], weights[w_source]).astype(BF16)

    tiles(src.shape[0], project_source)
    emb[...] = lax.dot_general(
        feat_ref[...], fw_ref[...], (((0,), (0,)), ((), ())), preferred_element_type=F32
    ).astype(BF16)
    loads[w_edge].wait()
    passed = 0
    for at in range(edges // TILE):
        if passed < CHUNKS:
            cast1.relay(passed)
            passed += 1
        here = pl.ds(at * TILE, TILE)
        hot = one_hot_rows(sender_ref[:, at * TILE : (at + 1) * TILE], src.shape[0])
        pre[here, :] = mm(emb[here, :], weights[w_edge]) + mm(hot, src[...])
    for at in range(passed, CHUNKS):
        cast1.relay(at)
    loads[w_edge2].wait()
    gather_near(cast1, tab1, slot_key, pre)

    for at in range(edges // TILE):
        here = pl.ds(at * TILE, TILE)
        hidden = silu(pre[here, :] + gather_far(tab1, slot_key, at)).astype(BF16)
        fresh[here, :] = (
            emb[here, :].astype(F32) + normalize(mm(hidden, weights[w_edge2]))
        ).astype(BF16)
    cast1.drain()

    jz = 2 * odd
    jy = 2 * (1 - odd)

    def partial(slot):
        return mm(one_hot_columns(slot_key, slot * rows, rows), fresh[...])

    pieces = [pl.ds(chunk * part, part) for chunk in range(CHUNKS)]
    sib_out[0] = partial(2 * jz + 1 - core).astype(BF16)
    sibs = []
    for chunk in range(CHUNKS):
        sibs.append(
            remote(
                sib_out.at[0, pieces[chunk]], sib_in.at[0, pieces[chunk]],
                sib_send.at[chunk], sib_recv.at[chunk], to_sib,
            )
        )
        sibs[-1].start()
    z_own[...] = partial(2 * jz + core)
    sib_out[1] = partial(2 * jy + 1 - core).astype(BF16)
    z_copies = []
    y_copies = []
    for chunk in range(CHUNKS):
        piece = pieces[chunk]
        sibs[chunk].wait_recv()
        z_out[piece, :] = (z_own[piece, :] + sib_in[0, piece, :].astype(F32)).astype(BF16)
        z_copies.append(
            remote(z_out.at[piece], z_in.at[piece], z_send.at[chunk], z_recv.at[chunk], to_fold)
        )
        z_copies[-1].start()
        y_copies.append(
            remote(y_out.at[piece], y_in.at[piece], y_send.at[chunk], y_recv.at[chunk], to_partner)
        )
    for at in (1, 2):
        if at == 2:
            sib_out[2] = partial(3 - core).astype(BF16)
        sibs.append(
            remote(
                sib_out.at[at], sib_in.at[at],
                sib_send.at[CHUNKS + at - 1], sib_recv.at[CHUNKS + at - 1], to_sib,
            )
        )
        sibs[-1].start()
    y_own[...] = partial(2 * jy + core)
    m_own[...] = partial(2 + core)
    sibs[CHUNKS].wait_recv()
    y_own[...] += sib_in[1].astype(F32)
    for at in (w_first, w_summed, w_second, w_link, w_lsrc, w_ldst, w_link2, w_vfirst, w_vsummed, w_vsecond):
        loads[at].wait()
    load_link.wait()
    cast2 = Multicast(tab2, 1)

    def forward(chunk):
        piece = pieces[chunk]
        z_copies[chunk].wait_recv()
        y_out[piece, :] = (y_own[piece, :] + z_in[piece, :].astype(F32)).astype(BF16)
        y_copies[chunk].start()

    def node(chunk):
        piece = pieces[chunk]
        y_copies[chunk].wait_recv()
        summed = (m_own[piece, :] + y_in[piece, :].astype(F32)).astype(BF16)
        hidden = silu(z_own[piece, :] + mm(summed, weights[w_summed])).astype(BF16)
        new = (
            mesh[piece, :].astype(F32) + normalize(mm(hidden, weights[w_second]))
        ).astype(BF16)
        mesh_next[piece, :] = new
        sends = pl.ds(pl.multiple_of((2 + core) * rows + chunk * part, part), part)
        tab2[sends, :] = mm(new, weights[w_lsrc]).astype(BF16)
        cast2.start(chunk)

    def project_link(at):
        link_pre[at, :] = mm(link[at, :], weights[w_link])

    forward(0)
    z_own[...] = mm(mesh[...], weights[w_first])
    sibs[CHUNKS + 1].wait_recv()
    m_own[...] += sib_in[2].astype(F32)
    for chunk in range(1, CHUNKS):
        forward(chunk)
        node(chunk - 1)
        if chunk > 2:
            cast2.relay(chunk - 3)
    node(CHUNKS - 1)
    tiles(edges, project_link)
    passed = max(CHUNKS - 3, 0)
    link_dst[...] = mm(mesh_next[...], weights[w_ldst]).astype(BF16)
    for at in range(edges // TILE):
        if passed < CHUNKS:
            cast2.relay(passed)
            passed += 1
        here = pl.ds(at * TILE, TILE)
        hot = one_hot_rows(link_receiver_ref[:, at * TILE : (at + 1) * TILE], rows)
        link_pre[here, :] += mm(hot, link_dst[...])
    for at in range(passed, CHUNKS):
        cast2.relay(at)
    y_own[...] = mm(mesh_next[...], weights[w_vfirst])
    total = 2 * patches
    bits = rows.bit_length() - 1
    sender = link_sender_ref[...]
    place = lax.shift_right_logical(sender, bits) - (2 * chip + core) + REACH
    place = jnp.where(place < 0, place + total, place)
    place = jnp.where(place >= total, place - total, place)
    link_key = (place + core) * rows + lax.bitwise_and(sender, rows - 1)
    gather_near(cast2, tab2, link_key, link_pre)

    for at in range(edges // TILE):
        here = pl.ds(at * TILE, TILE)
        hidden = silu(link_pre[here, :] + gather_far(tab2, link_key, at)).astype(BF16)
        fresh[here, :] = (
            link[here, :].astype(F32) + normalize(mm(hidden, weights[w_link2]))
        ).astype(BF16)
    link_sum = mm(one_hot_columns(link_receiver_ref[...], 0, rows), fresh[...]).astype(BF16)
    hidden = silu(y_own[...] + mm(link_sum, weights[w_vsummed])).astype(BF16)
    out_ref[...] = (
        mesh_next[...].astype(F32) + normalize(mm(hidden, weights[w_vsecond]))
    ).astype(BF16)
    cast2.drain()
    for copy in sibs + z_copies + y_copies:
        copy.wait_send()


def body(
    patches,
    grid_latent, mesh_latent, edge_features, edge_sender, edge_receiver, block_offset,
    link_latent, link_sender, link_receiver, feature_weight, source_weight, target_weight,
    edge_weight, edge_second, node_first, node_summed, node_second, link_weight, link_source,
    link_target, link_second, vertex_first, vertex_summed, vertex_second,
):
    rows, width = mesh_latent.shape
    edges = edge_sender.shape[0]
    vmem = pl.BlockSpec(memory_space=pltpu.VMEM)
    smem = pl.BlockSpec(memory_space=pltpu.SMEM)
    anywhere = pl.BlockSpec(memory_space=pltpu.HBM)
    dma = pltpu.SemaphoreType.DMA
    table = pltpu.VMEM((6 * rows, width), BF16)
    flat = pltpu.VMEM((rows, width), BF16)
    return pl.pallas_call(
        functools.partial(kernel, patches),
        out_shape=jax.ShapeDtypeStruct((rows, width), BF16),
        in_specs=[vmem, vmem, vmem, smem, vmem, vmem, vmem] + [anywhere] * (3 + WEIGHTS),
        out_specs=vmem,
        scratch_shapes=[
            pltpu.VMEM(grid_latent.shape, BF16),
            flat,
            pltpu.VMEM(link_latent.shape, BF16),
            pltpu.VMEM((WEIGHTS, width, width), BF16),
            table,
            table,
            pltpu.VMEM((grid_latent.shape[0], width), BF16),
            pltpu.VMEM((edges, width), BF16),
            pltpu.VMEM((edges, width), F32),
            pltpu.VMEM((edges, width), F32),
            pltpu.VMEM((edges, width), BF16),
            pltpu.VMEM((3, rows, width), BF16),
            pltpu.VMEM((3, rows, width), BF16),
            flat, flat, flat, flat,
            pltpu.VMEM((rows, width), F32),
            pltpu.VMEM((rows, width), F32),
            pltpu.VMEM((rows, width), F32),
            flat, flat,
            dma((WEIGHTS + 3,)),
            dma((2, 5 * CHUNKS)), dma((2, 5 * CHUNKS)),
            dma((CHUNKS + 2,)), dma((CHUNKS + 2,)),
            dma((CHUNKS,)), dma((CHUNKS,)),
            dma((CHUNKS,)), dma((CHUNKS,)),
        ],
        compiler_params=pltpu.CompilerParams(
            collective_id=0, has_side_effects=True, vmem_limit_bytes=62 * 1024 * 1024
        ),
    )(
        edge_features, edge_sender.reshape(1, -1), edge_receiver.reshape(1, -1), block_offset,
        link_sender.reshape(1, -1), link_receiver.reshape(1, -1), feature_weight,
        grid_latent, mesh_latent, link_latent,
        target_weight, source_weight, edge_weight, edge_second, node_first, node_summed,
        node_second, link_weight, link_source, link_target, link_second, vertex_first,
        vertex_summed, vertex_second,
    )


def solution(mesh):
    rows = P(AXES, None)
    flat = P(AXES)
    placed = (rows, rows, P(None, AXES), flat, flat, flat, rows, flat, flat) + (P(),) * 15
    return jax.shard_map(
        functools.partial(body, mesh.shape["patch"]),
        mesh=mesh,
        in_specs=placed,
        out_specs=rows,
        check_vma=False,
    )
```
